32 devices in a mesh: member: 2 (over x), lat: 16 (over z, y, core).
Axes of the slice: x: 2, y: 2, z: 4, core: 2. Of those that a mesh axis runs over, the one named last changes fastest.
Arguments:
- state: float32 [10, 128, 128, 256], P('member', None, 'lat'), parts along dimension 0, may hold values from -6 to 6
- wind: float32 [256, 128, 256], P('member', 'lat'), parts along dimension 0, may hold values from -0.9 to 0.9
- sunlight: float32 [256, 256], P(('member', 'lat')), parts along dimension 0, may hold values from 0.1 to 1
- day_list: int32 [32, 16], P(('member', 'lat')), parts along dimension 0, may hold values from -1 to 15, as said below
- w_first: bfloat16 [640, 2048], replicated, may hold values from -0.25 to 0.25
- bias: float32 [2048], replicated, may hold values from -3 to 3
- w_second: bfloat16 [2048, 128], replicated, may hold values from -0.125 to 0.125
- remap: float32 [128, 128], replicated, may hold values from -1.5 to 2
Outputs:
- new_state: float32 [10, 128, 128, 256], P('member', None, 'lat'), parts along dimension 0
The draws below stay inside these ranges and needn't reach their ends.
There are 2 independent parts, one for each index of `member`. The reference program is written for one: setup_inputs(seed, part) draws one part's arguments, and reference() takes and returns one part's arrays. A program takes and returns all parts, laid end to end along the dimension named above; an argument that names none is the same for every part. Nothing has to cross between parts.
Inputs may be any that keep to these rules, and one draw needn't show every extreme that they name: `day_list`: row d names the daylit blocks of band d, each once, as a cyclic run of consecutive numbers placed first, then -1; every row names at least one block. Rows d and d + 8 together name at most 20 blocks; row 0 names all 16 and row 8 exactly 4.
All inputs are finite; a program needn't handle non-finite values.
Results may differ from the reference program's by a relative error of at most 0.00062.
Values may be sent and summed in bfloat16 or wider, within the bound.
A program may use at most 128 MiB of HBM per device.

```python
import math
import jax
import jax.numpy as jnp
from jax import lax

FIELDS = 5
LEV = 128
HID = 2048
NLON = 256
COLBLK = 128
STEPS = 2
BANDS = 16
NLAT = 128
BLK_DEV = 16


def draw_day_list(key, part):
    half = BANDS // 2
    band = jnp.arange(half, dtype=jnp.int32)
    key_a, key_b, key_c = jax.random.split(key, 3)
    north_cut = jax.random.randint(key_a, (half,), 0, 2, dtype=jnp.int32)
    south_cut = jax.random.randint(key_b, (half,), 0, 2, dtype=jnp.int32)
    north_cut = jnp.where(band == 0, 0, north_cut)
    south_cut = jnp.where(band == 0, 0, south_cut)
    north_less = jnp.minimum(BLK_DEV // 2, band * BLK_DEV // BANDS + north_cut)
    north_count = BLK_DEV - north_less
    south_count = BLK_DEV // 4 + north_less - south_cut
    south_count = jnp.maximum(south_count, 1)
    counts = jnp.concatenate([north_count, south_count])
    starts = jax.random.randint(key_c, (BANDS,), 0, BLK_DEV, dtype=jnp.int32)
    position = jnp.arange(BLK_DEV, dtype=jnp.int32)
    listed = (starts[:, None] + position[None, :]) % BLK_DEV
    return jnp.where(position[None, :] < counts[:, None], listed, -1).astype(jnp.int32)


def draw_remap(key, part):
    noise = jax.random.normal(key, (LEV, LEV), jnp.float32) * (0.5 / math.sqrt(LEV))
    return 0.7 * jnp.eye(LEV, dtype=jnp.float32) + noise


def block_scale(rng, extent, cuts, low, top_value):
    level, own = 1.0, jax.random.fold_in(rng, 6)
    for dim, shards_of in cuts:
        draws = jnp.exp(jax.random.uniform(jax.random.fold_in(own, dim), (shards_of,), jnp.float32, low / len(cuts), top_value / len(cuts)))
        level = level * jnp.repeat(draws, extent[dim] // shards_of).reshape([-1 if axis == dim else 1 for axis in range(len(extent))])
    return level


def scatter_about(stream_key, dims, deviation, reach, pieces=(), kind=jnp.bfloat16):
    values = deviation * jax.random.normal(stream_key, dims, jnp.float32)
    if pieces:
        values = values * block_scale(stream_key, dims, pieces, -0.22, 0.18)
    return jnp.clip(values, -reach, reach).astype(kind)


def setup_inputs(seed: int = 0, part: int = 0) -> dict:
    streams_of = jax.random.split(jax.random.key(seed), 9)
    part_keys = jax.random.split(jax.random.fold_in(streams_of[8], part), 9)
    state = scatter_about(part_keys[0], (FIELDS, LEV, NLAT, NLON), 1.0, 6.0, ((2, 16),), jnp.float32)
    wind = jnp.clip(jax.random.uniform(part_keys[1], (LEV, NLAT, NLON), jnp.float32, -0.9, 0.9) * block_scale(part_keys[1], (LEV, NLAT, NLON), ((1, 16),), -0.4, 0.0), -0.9, 0.9)
    sunlight = jnp.clip(0.1 + 0.9 * jax.random.uniform(part_keys[2], (NLAT, NLON), jnp.float32) ** block_scale(part_keys[2], (NLAT, NLON), ((0, 16),), -0.2, 0.2), 0.1, 1.0)
    day_list = draw_day_list(jax.random.fold_in(jax.random.fold_in(streams_of[8], part), 71), part)
    w_first = scatter_about(streams_of[4], (FIELDS * LEV, HID), (FIELDS * LEV) ** -0.5, 0.25)
    bias = scatter_about(streams_of[5], (HID,), 0.5, 3.0, (), jnp.float32)
    w_second = scatter_about(streams_of[6], (HID, LEV), HID ** -0.5, 0.125)
    remap = draw_remap(jax.random.fold_in(streams_of[8], 71), part)
    return dict(state=state, wind=wind, sunlight=sunlight, day_list=day_list, w_first=w_first, bias=bias, w_second=w_second, remap=remap)


def min_mod(left, right):
    return 0.5 * (jnp.sign(left) + jnp.sign(right)) * jnp.minimum(jnp.abs(left), jnp.abs(right))


def advance(padded, courant):
    length = padded.shape[2] - 4
    slopes = min_mod(padded[:, :, 2:] - padded[:, :, 1:-1], padded[:, :, 1:-1] - padded[:, :, :-2])
    upper_q = padded[:, :, 1:length + 2]
    upper_s = slopes[:, :, 0:length + 1]
    lower_q = padded[:, :, 2:length + 3]
    lower_s = slopes[:, :, 1:length + 2]
    speed = courant[None]
    fluxes = jnp.where(speed > 0.0, speed * (upper_q + 0.5 * (1.0 - speed) * upper_s), speed * (lower_q - 0.5 * (1.0 + speed) * lower_s))
    return padded[:, :, 2:length + 2] - (fluxes[:, :, 1:] - fluxes[:, :, :-1])


def reference(state, wind, sunlight, day_list, w_first, bias, w_second, remap):
    current = state
    courant = jnp.concatenate([wind, jnp.zeros_like(wind[:, :1])], axis=1)
    for step in range(STEPS):
        padded = jnp.pad(current, ((0, 0), (0, 0), (2, 2), (0, 0)))
        current = advance(padded, courant)
    columns = current.reshape(FIELDS, LEV, NLAT * NLON)
    remapped = jnp.einsum("km,fmc->fkc", remap, columns, precision=lax.Precision.HIGHEST)
    inputs = remapped.astype(jnp.bfloat16).reshape(FIELDS, LEV, NLAT, NLON)
    rows_first = jnp.moveaxis(inputs, 2, 0)
    w_shaped = w_first.astype(jnp.float32).reshape(FIELDS, LEV, HID)
    w_out = w_second.astype(jnp.float32)

    def one_row(row):
        hidden = jnp.einsum("flc,flh->ch", row.astype(jnp.float32), w_shaped, precision=lax.Precision.HIGHEST) + bias
        hidden = jax.nn.gelu(hidden, approximate=True).astype(jnp.bfloat16)
        return jnp.dot(hidden.astype(jnp.float32), w_out, precision=lax.Precision.HIGHEST).T

    net = lax.map(one_row, rows_first)
    daylit = jnp.any(day_list[:, None, :] == jnp.arange(BLK_DEV, dtype=jnp.int32)[None, :, None], axis=2)
    daylit = jnp.repeat(daylit.astype(jnp.float32), COLBLK, axis=1).reshape(NLAT, NLON)
    heating = jnp.moveaxis(net, 1, 0) * (daylit * sunlight)[None]
    heating = heating.reshape(1, LEV, NLAT * NLON)
    output = jnp.concatenate([remapped[:1] + heating, remapped[1:]], axis=0)
    return output.reshape(FIELDS, LEV, NLAT, NLON)
```

```python
import functools

import jax
import jax.numpy as jnp
from jax import lax
from jax.experimental import pallas as pl
from jax.experimental.pallas import tpu as pltpu
from jax.sharding import PartitionSpec as P

STEPS = 2
REACH = 2 * STEPS
SCALE = 4096.0
PARTS = 2
CHUNKS = 4
MIB = 1 << 20


def pack_kernel(state_ref, wind_ref, up_ref, down_ref):
    fields, levels, rows, lons = state_ref.shape
    flat = state_ref.reshape(fields * levels * rows, lons)
    winds = wind_ref.reshape(levels * rows, lons)
    for k in range(REACH):
        for f in range(fields):
            base = f * levels * rows
            up_ref[0, k * fields + f] = flat[pl.ds(base + rows - REACH + k, levels, stride=rows), :] * SCALE
            down_ref[0, k * fields + f] = flat[pl.ds(base + k, levels, stride=rows), :] * SCALE
    for k in range(2):
        up_ref[0, REACH * fields + k] = winds[pl.ds(rows - 2 + k, levels, stride=rows), :] * SCALE
    for k in range(3):
        down_ref[0, REACH * fields + k] = winds[pl.ds(k, levels, stride=rows), :] * SCALE


def pack(state, wind):
    fields, levels, rows, lons = state.shape
    part = lons // PARTS
    step = levels // CHUNKS
    slabs = REACH * fields
    return pl.pallas_call(
        pack_kernel,
        grid=(PARTS, CHUNKS),
        in_specs=[
            pl.BlockSpec((fields, step, rows, part), lambda h, i: (0, i, 0, h)),
            pl.BlockSpec((step, rows, part), lambda h, i: (i, 0, h)),
        ],
        out_specs=[
            pl.BlockSpec((1, slabs + 2, step, part), lambda h, i: (h, 0, i, 0)),
            pl.BlockSpec((1, slabs + 3, step, part), lambda h, i: (h, 0, i, 0)),
        ],
        out_shape=[
            jax.ShapeDtypeStruct((PARTS, slabs + 2, levels, part), jnp.float32),
            jax.ShapeDtypeStruct((PARTS, slabs + 3, levels, part), jnp.float32),
        ],
        name="pack",
        compiler_params=pltpu.CompilerParams(vmem_limit_bytes=40 * MIB),
        cost_estimate=pl.CostEstimate(flops=10**6, bytes_accessed=12 * 10**6, transcendentals=0),
    )(state, wind)


def limited(left, right):
    return jnp.maximum(jnp.minimum(left, right), 0.0) + jnp.minimum(jnp.maximum(left, right), 0.0)


def advance(q, c, ck, positive, first, last):
    diff = {j: q[j + 1] - q[j] for j in range(first - 2, last + 2)}
    slope = {j: limited(diff[j], diff[j - 1]) for j in range(first - 1, last + 2)}
    flux = {}
    for j in range(first, last + 2):
        flux[j] = c[j] * jnp.where(positive[j], q[j - 1], q[j]) + ck[j] * jnp.where(
            positive[j], slope[j - 1], slope[j]
        )
    return {j: q[j] - (flux[j + 1] - flux[j]) for j in range(first, last + 1)}


def gelu(v):
    inner = v * (0.7978845608028654 + (0.7978845608028654 * 0.044715) * (v * v))
    half = 0.5 * v
    return (half + half * jnp.tanh(inner)).astype(jnp.bfloat16)


def main_kernel(part, flags, state_ref, wind_ref, north_ref, south_ref, sun_ref, bias_ref,
                remap_ref, w1_hbm, w2_hbm, *rest):
    out_ref, adv, x16, w1, w2, sems = rest[-6:]
    step_id = pl.program_id(0)
    fields, chunk, rows, lons = state_ref.shape
    levels = adv.shape[2]
    slabs = REACH * fields
    load_1 = pltpu.make_async_copy(w1_hbm, w1, sems.at[0])
    load_2 = pltpu.make_async_copy(w2_hbm, w2, sems.at[1])

    @pl.when(step_id == 0)
    def _():
        load_1.start()
        load_2.start()

    @pl.when(step_id < CHUNKS)
    def _():
        flat = state_ref.reshape(fields * chunk * rows, lons)
        winds = wind_ref.reshape(chunk * rows, lons)
        inner = jnp.where(flags[flags.shape[0] - 1] > 0, 1.0, 0.0)

        @pl.loop(0, chunk // 8)
        def _(t):
            here = pl.ds(pl.multiple_of(t * 8, 8), 8)
            there = pl.ds(pl.multiple_of(step_id * chunk + t * 8, 8), 8)
            c = {}
            for j in range(-2, rows + 3):
                if j < 0:
                    c[j] = north_ref[slabs + 2 + j, here, :]
                elif j < rows:
                    c[j] = winds[pl.ds(t * 8 * rows + j, 8, stride=rows), :]
                else:
                    c[j] = south_ref[slabs + j - rows, here, :]
            positive = {j: v > 0.0 for j, v in c.items()}
            ck = {j: 0.5 * (jnp.abs(v) - v * v) for j, v in c.items()}
            for f in range(fields):
                q = {}
                for j in range(-REACH, rows + REACH):
                    if j < 0:
                        q[j] = north_ref[(j + REACH) * fields + f, here, :]
                    elif j < rows:
                        q[j] = flat[pl.ds(f * chunk * rows + t * 8 * rows + j, 8, stride=rows), :]
                    else:
                        q[j] = south_ref[(j - rows) * fields + f, here, :]
                q = advance(q, c, ck, positive, -2, rows + 1)
                q[-1] = q[-1] * inner
                q[-2] = q[-2] * inner
                q = advance(q, c, ck, positive, 0, rows - 1)
                for j in range(rows):
                    adv[j, f, there, :] = q[j]

    @pl.when(step_id == CHUNKS)
    def _():
        load_1.wait()
        load_2.wait()
        flat_out = out_ref.reshape(fields * levels * rows, lons)
        remap = remap_ref[...]
        r_high = remap.astype(jnp.bfloat16)
        r_low = (remap - r_high.astype(jnp.float32)).astype(jnp.bfloat16)
        r_all = jnp.concatenate([r_high, r_low, r_high], axis=1)
        hidden_size = w1.shape[0]
        tile = hidden_size // 4

        for pair in range(rows // 2):
            a, b = 2 * pair, 2 * pair + 1
            for f in range(fields):
                x = jnp.concatenate([adv[a, f], adv[b, f]], axis=1)
                high = x.astype(jnp.bfloat16)
                low = (x - high.astype(jnp.float32)).astype(jnp.bfloat16)
                stacked = jnp.concatenate([high, high, low], axis=0)
                y = jnp.dot(r_all, stacked, preferred_element_type=jnp.float32)
                x16[pl.ds(f * levels, levels), :] = y.astype(jnp.bfloat16)
                flat_out[pl.ds(f * levels * rows + a, levels, stride=rows), :] = y[:, :lons]
                flat_out[pl.ds(f * levels * rows + b, levels, stride=rows), :] = y[:, lons:]
            lit_a = flags[PARTS * a + part]
            lit_b = flags[PARTS * b + part]

            @pl.when(lit_a + lit_b > 0)
            def _():
                inputs = x16[...]

                def layer(t):
                    z = jnp.dot(w1[pl.ds(t * tile, tile), :], inputs,
                                preferred_element_type=jnp.float32)
                    wide = bias_ref[pl.ds(t * tile, tile), :]
                    return z + jnp.concatenate([wide, wide], axis=1)

                net = jnp.zeros((levels, 2 * lons), jnp.float32)
                z = layer(0)
                for t in range(4):
                    later = layer(t + 1) if t < 3 else None
                    net = net + jnp.dot(w2[:, pl.ds(t * tile, tile)], gelu(z),
                                        preferred_element_type=jnp.float32)
                    z = later
                for r, lit, values in ((a, lit_a, net[:, :lons]), (b, lit_b, net[:, lons:])):
                    weight = sun_ref[pl.ds(r, 1), :] * jnp.where(lit > 0, 1.0, 0.0)
                    place = pl.ds(r, levels, stride=rows)
                    flat_out[place, :] = flat_out[place, :] + weight * values


def compute(part, flags, state, wind, north, south, sunlight, bias, remap, w1, w2, before):
    fields, levels, rows, lons = state.shape
    width = lons // PARTS
    step = levels // CHUNKS
    last = CHUNKS - 1
    hidden_size = w1.shape[0]
    any_spec = pl.BlockSpec(memory_space=pl.ANY)
    in_specs = [
        pl.BlockSpec((fields, step, rows, width), lambda i, s: (0, jnp.minimum(i, last), 0, part)),
        pl.BlockSpec((step, rows, width), lambda i, s: (jnp.minimum(i, last), 0, part)),
        pl.BlockSpec((north.shape[0], step, width), lambda i, s: (0, jnp.minimum(i, last), 0)),
        pl.BlockSpec((south.shape[0], step, width), lambda i, s: (0, jnp.minimum(i, last), 0)),
        pl.BlockSpec((rows, width), lambda i, s: (0, part)),
        pl.BlockSpec((hidden_size, width), lambda i, s: (0, 0)),
        pl.BlockSpec((levels, levels), lambda i, s: (0, 0)),
        any_spec,
        any_spec,
    ]
    operands = [flags, state, wind, north, south, sunlight, bias, remap, w1, w2]
    aliases = {}
    if before is not None:
        in_specs.append(any_spec)
        operands.append(before)
        aliases = {len(operands) - 1: 0}
    return pl.pallas_call(
        functools.partial(main_kernel, part),
        grid_spec=pltpu.PrefetchScalarGridSpec(
            num_scalar_prefetch=1,
            grid=(CHUNKS + 1,),
            in_specs=in_specs,
            out_specs=pl.BlockSpec((fields, levels, rows, width), lambda i, s: (0, 0, 0, part)),
            scratch_shapes=[
                pltpu.VMEM((rows, fields, levels, width), jnp.float32),
                pltpu.VMEM((fields * levels, 2 * width), jnp.bfloat16),
                pltpu.VMEM(w1.shape, jnp.bfloat16),
                pltpu.VMEM(w2.shape, jnp.bfloat16),
                pltpu.SemaphoreType.DMA((2,)),
            ],
        ),
        out_shape=jax.ShapeDtypeStruct(state.shape, jnp.float32),
        input_output_aliases=aliases,
        name="column_step",
        compiler_params=pltpu.CompilerParams(vmem_limit_bytes=48 * MIB),
        cost_estimate=pl.CostEstimate(flops=4 * 10**9, bytes_accessed=12 * 10**6, transcendentals=2 * 10**6),
    )(*operands)


def shards(state, wind, sunlight, day_list, w_first, bias, w_second, remap):
    count = lax.axis_size("lat")
    upward = [(i, i + 1) for i in range(count - 1)]
    downward = [(i + 1, i) for i in range(count - 1)]
    up, down = pack(state, wind)
    halos = []
    for part in range(PARTS):
        north = lax.ppermute(up[part].astype(jnp.float16), "lat", upward)
        south = lax.ppermute(down[part].astype(jnp.float16), "lat", downward)
        halos.append((north, south))
    blocks = day_list.shape[1]
    block_ids = jnp.arange(blocks, dtype=jnp.int32)
    lit = jnp.any(day_list[0][None, :] == block_ids[:, None], axis=1).astype(jnp.int32)
    inner = (lax.axis_index("lat") > 0).astype(jnp.int32)
    flags = jnp.concatenate([lit, inner[None]])
    w1, w2 = w_first.T, w_second.T
    wide_bias = jnp.broadcast_to(bias[:, None], (bias.shape[0], state.shape[3] // PARTS))
    out = None
    for part in range(PARTS):
        north, south = [h.astype(jnp.float32) * (1.0 / SCALE) for h in halos[part]]
        out = compute(part, flags, state, wind, north, south, sunlight, wide_bias, remap, w1, w2, out)
    return out


def solution(mesh):
    placed = (
        P("member", None, "lat", None),
        P("member", "lat", None),
        P(("member", "lat"), None),
        P(("member", "lat"), None),
        P(),
        P(),
        P(),
        P(),
    )
    return jax.shard_map(
        shards,
        mesh=mesh,
        in_specs=placed,
        out_specs=P("member", None, "lat", None),
        check_vma=False,
    )
```

```python
import functools

import jax
import jax.numpy as jnp
from jax import lax
from jax.experimental import pallas as pl
from jax.experimental.pallas import tpu as pltpu
from jax.sharding import PartitionSpec as P

STEPS = 2
REACH = 2 * STEPS
SCALE = 4096.0
FACES = 3
PARTS = 2
CHUNKS = 4
TILES = 4
MIB = 1 << 20


def pack_kernel(flags, state_ref, wind_ref, *rest, slow, scale):
    sent_ref = rest[-1]
    fields, levels, rows, lons = state_ref.shape
    flat = state_ref.reshape(fields * levels * rows, lons)
    winds = wind_ref.reshape(levels * rows, lons)
    odd = flags[flags.shape[0] - 2]
    upward = odd if slow else 1 - odd
    for k in range(REACH):
        for f in range(fields):
            start = f * levels * rows + upward * (rows - REACH) + k
            sent_ref[k * fields + f] = flat[pl.ds(start, levels, stride=rows), :] * scale
    for k in range(FACES):
        start = upward * (rows - FACES) + k
        sent_ref[REACH * fields + k] = winds[pl.ds(start, levels, stride=rows), :] * scale


def pack(flags, state, wind, slow, scale, first, count, after):
    fields, levels, rows, lons = state.shape
    part = lons // PARTS
    step = levels // CHUNKS
    slabs = REACH * fields + FACES
    return pl.pallas_call(
        functools.partial(pack_kernel, slow=slow, scale=scale),
        grid_spec=pltpu.PrefetchScalarGridSpec(
            num_scalar_prefetch=1,
            grid=(count, CHUNKS),
            in_specs=[
                pl.BlockSpec((fields, step, rows, part), lambda h, i, s: (0, i, 0, first + h)),
                pl.BlockSpec((step, rows, part), lambda h, i, s: (i, 0, first + h)),
            ] + [pl.BlockSpec(memory_space=pl.ANY)] * len(after),
            out_specs=pl.BlockSpec((slabs, step, part), lambda h, i, s: (0, i, h)),
        ),
        out_shape=jax.ShapeDtypeStruct((slabs, levels, count * part), jnp.float32),
        name="pack",
        compiler_params=pltpu.CompilerParams(vmem_limit_bytes=48 * MIB),
        cost_estimate=pl.CostEstimate(flops=1000, bytes_accessed=1000, transcendentals=0),
    )(flags, state, wind, *after)


def limited(left, right):
    return jnp.maximum(jnp.minimum(left, right), 0.0) + jnp.minimum(jnp.maximum(left, right), 0.0)


def advance(q, c, ck, positive, first, last):
    diff = {j: q[j + 1] - q[j] for j in range(first - 2, last + 2)}
    slope = {j: limited(diff[j], diff[j - 1]) for j in range(first - 1, last + 2)}
    flux = {}
    for j in range(first, last + 2):
        flux[j] = c[j] * jnp.where(positive[j], q[j - 1], q[j]) + ck[j] * jnp.where(
            positive[j], slope[j - 1], slope[j]
        )
    return {j: q[j] - (flux[j + 1] - flux[j]) for j in range(first, last + 1)}


def gelu(v):
    inner = v * (0.7978845608028654 + (0.7978845608028654 * 0.044715) * (v * v))
    half = 0.5 * v
    return (half + half * jnp.tanh(inner)).astype(jnp.bfloat16)


def advect_rows(north, inner, state_ref, wind_ref, halo_ref, adv, offset):
    fields, chunk, rows, lons = state_ref.shape
    slabs = REACH * fields
    flat = state_ref.reshape(fields * chunk * rows, lons)
    winds = wind_ref.reshape(chunk * rows, lons)
    first = 0 if north else rows - REACH
    last = first + REACH - 1

    @pl.loop(0, chunk // 8)
    def _(t):
        here = pl.ds(pl.multiple_of(t * 8, 8), 8)
        there = pl.ds(pl.multiple_of(offset + t * 8, 8), 8)
        c = {}
        for j in range(first - 2, last + 4):
            if j < 0:
                c[j] = halo_ref[slabs + FACES + j, here, :]
            elif j < rows:
                c[j] = winds[pl.ds(t * 8 * rows + j, 8, stride=rows), :]
            else:
                c[j] = halo_ref[slabs + j - rows, here, :]
        positive = {j: v > 0.0 for j, v in c.items()}
        ck = {j: 0.5 * (jnp.abs(v) - v * v) for j, v in c.items()}
        for f in range(fields):
            q = {}
            for j in range(first - REACH, last + REACH + 1):
                if j < 0:
                    q[j] = halo_ref[(j + REACH) * fields + f, here, :]
                elif j < rows:
                    q[j] = flat[pl.ds(f * chunk * rows + t * 8 * rows + j, 8, stride=rows), :]
                else:
                    q[j] = halo_ref[(j - rows) * fields + f, here, :]
            q = advance(q, c, ck, positive, first - 2, last + 2)
            if north:
                q[-1] = q[-1] * inner
                q[-2] = q[-2] * inner
            q = advance(q, c, ck, positive, first, last)
            for j in range(REACH):
                adv[j, f, there, :] = q[first + j]


def main_kernel(slow, part, flags, state_ref, wind_ref, halo_ref, sun_ref, bias_ref,
                remap_ref, w1_hbm, w2_hbm, *rest):
    if slow:
        out_ref, adv, x16, w1, w2, sems = rest[-6:]
    else:
        out_ref, unscale_ref, adv, x16, w1, w2, sems = rest[-7:]
        unscale_ref[...] = jnp.full(unscale_ref.shape, 1.0 / SCALE, jnp.float32)
    half = pl.program_id(0)
    step_id = pl.program_id(1)
    fields, chunk, rows, lons = state_ref.shape
    levels = adv.shape[2]
    load_1 = pltpu.make_async_copy(w1_hbm, w1, sems.at[0])
    load_2 = pltpu.make_async_copy(w2_hbm, w2, sems.at[1])
    odd = flags[flags.shape[0] - 2]
    north = 1 - odd if slow else odd
    inner = jnp.where(flags[flags.shape[0] - 1] > 0, 1.0, 0.0)
    offset = step_id * chunk

    @pl.when((step_id == 0) & (half == 0))
    def _():
        load_1.start()
        load_2.start()

    @pl.when((step_id < CHUNKS) & (north == 1))
    def _():
        advect_rows(True, inner, state_ref, wind_ref, halo_ref, adv, offset)

    @pl.when((step_id < CHUNKS) & (north == 0))
    def _():
        advect_rows(False, inner, state_ref, wind_ref, halo_ref, adv, offset)

    @pl.when((step_id == CHUNKS) & (half == 0))
    def _():
        load_1.wait()
        load_2.wait()

    @pl.when(step_id == CHUNKS)
    def _():
        base = (1 - north) * (rows - REACH)
        if slow:
            flat_out = out_ref.reshape(fields * levels * rows, lons)
            fast_ref = rest[0]
            fast_base = north * (rows - REACH)
            for k in range(REACH):
                for f in range(fields):
                    place = pl.ds(f * levels * rows + fast_base + k, levels, stride=rows)
                    flat_out[place, :] = fast_ref[k, f]

        def put(k, f, values):
            if slow:
                flat_out[pl.ds(f * levels * rows + base + k, levels, stride=rows), :] = values
            else:
                out_ref[k, f] = values

        def get(k, f):
            if slow:
                return flat_out[pl.ds(f * levels * rows + base + k, levels, stride=rows), :]
            return out_ref[k, f]

        remap = remap_ref[...]
        r_high = remap.astype(jnp.bfloat16)
        r_low = (remap - r_high.astype(jnp.float32)).astype(jnp.bfloat16)
        r_all = jnp.concatenate([r_high, r_low, r_high], axis=1)
        hidden_size = w1.shape[0]
        tile = hidden_size // TILES

        for pair in range(REACH // 2):
            a, b = 2 * pair, 2 * pair + 1
            for f in range(fields):
                x = jnp.concatenate([adv[a, f], adv[b, f]], axis=1)
                high = x.astype(jnp.bfloat16)
                low = (x - high.astype(jnp.float32)).astype(jnp.bfloat16)
                stacked = jnp.concatenate([high, high, low], axis=0)
                y = jnp.dot(r_all, stacked, preferred_element_type=jnp.float32)
                x16[pl.ds(f * levels, levels), :] = y.astype(jnp.bfloat16)
                put(a, f, y[:, :lons])
                put(b, f, y[:, lons:])
            lit_a = flags[PARTS * (base + a) + part + half]
            lit_b = flags[PARTS * (base + b) + part + half]

            @pl.when(lit_a + lit_b > 0)
            def _():
                inputs = x16[...]

                def layer(t):
                    z = jnp.dot(w1[pl.ds(t * tile, tile), :], inputs,
                                preferred_element_type=jnp.float32)
                    wide = bias_ref[pl.ds(t * tile, tile), :]
                    return z + jnp.concatenate([wide, wide], axis=1)

                net = jnp.zeros((levels, 2 * lons), jnp.float32)
                z = layer(0)
                for t in range(TILES):
                    later = layer(t + 1) if t < TILES - 1 else None
                    net = net + jnp.dot(w2[:, pl.ds(t * tile, tile)], gelu(z),
                                        preferred_element_type=jnp.float32)
                    z = later
                for k, lit, values in ((a, lit_a, net[:, :lons]), (b, lit_b, net[:, lons:])):
                    weight = sun_ref[pl.ds(base + k, 1), :] * jnp.where(lit > 0, 1.0, 0.0)
                    put(k, 0, get(k, 0) + weight * values)


def compute(slow, part, flags, state, wind, halo, sunlight, bias, remap, w1, w2, fast=None, before=None):
    fields, levels, rows, lons = state.shape
    width = lons // PARTS
    step = levels // CHUNKS
    last = CHUNKS - 1
    hidden_size = w1.shape[0]
    any_spec = pl.BlockSpec(memory_space=pl.ANY)
    halves = 1 if slow else PARTS
    in_specs = [
        pl.BlockSpec((fields, step, rows, width), lambda h, i, s: (0, jnp.minimum(i, last), 0, part + h)),
        pl.BlockSpec((step, rows, width), lambda h, i, s: (jnp.minimum(i, last), 0, part + h)),
        pl.BlockSpec((halo.shape[0], step, width), lambda h, i, s: (0, jnp.minimum(i, last), h)),
        pl.BlockSpec((rows, width), lambda h, i, s: (0, part + h)),
        pl.BlockSpec((hidden_size, width), lambda h, i, s: (0, 0)),
        pl.BlockSpec((levels, levels), lambda h, i, s: (0, 0)),
        any_spec,
        any_spec,
    ]
    operands = [flags, state, wind, halo, sunlight, bias, remap, w1, w2]
    aliases = {}
    if slow:
        in_specs.append(pl.BlockSpec((REACH, fields, levels, width), lambda h, i, s: (0, 0, 0, part)))
        operands.append(fast)
        out_spec = pl.BlockSpec((fields, levels, rows, width), lambda h, i, s: (0, 0, 0, part))
        out_shape = jax.ShapeDtypeStruct(state.shape, jnp.float32)
        if before is not None:
            in_specs.append(any_spec)
            operands.append(before)
            aliases = {len(operands) - 1: 0}
    else:
        out_spec = [
            pl.BlockSpec((REACH, fields, levels, width), lambda h, i, s: (0, 0, 0, h)),
            pl.BlockSpec((8, width), lambda h, i, s: (0, 0)),
        ]
        out_shape = [
            jax.ShapeDtypeStruct((REACH, fields, levels, lons), jnp.float32),
            jax.ShapeDtypeStruct((8, width), jnp.float32),
        ]
    return pl.pallas_call(
        functools.partial(main_kernel, slow, part),
        grid_spec=pltpu.PrefetchScalarGridSpec(
            num_scalar_prefetch=1,
            grid=(halves, CHUNKS + 1),
            in_specs=in_specs,
            out_specs=out_spec,
            scratch_shapes=[
                pltpu.VMEM((REACH, fields, levels, width), jnp.float32),
                pltpu.VMEM((fields * levels, 2 * width), jnp.bfloat16),
                pltpu.VMEM(w1.shape, jnp.bfloat16),
                pltpu.VMEM(w2.shape, jnp.bfloat16),
                pltpu.SemaphoreType.DMA((2,)),
            ],
        ),
        out_shape=out_shape,
        input_output_aliases=aliases,
        name="slow_rows" if slow else "fast_rows",
        compiler_params=pltpu.CompilerParams(vmem_limit_bytes=40 * MIB),
        cost_estimate=pl.CostEstimate(
            flops=2 * 10**9 * halves, bytes_accessed=6 * 10**6 * halves, transcendentals=10**6 * halves
        ),
    )(*operands)


def shards(state, wind, sunlight, day_list, w_first, bias, w_second, remap):
    count = lax.axis_size("lat")
    near = [(i, i ^ 1) for i in range(count) if i ^ 1 < count]
    far = [(i, i + 1) for i in range(1, count - 1, 2)]
    far = far + [(j, i) for i, j in far]
    index = lax.axis_index("lat")
    blocks = day_list.shape[1]
    block_ids = jnp.arange(blocks, dtype=jnp.int32)
    lit = jnp.any(day_list[0][None, :] == block_ids[:, None], axis=1).astype(jnp.int32)
    odd = (index % 2).astype(jnp.int32)
    inner = (index > 0).astype(jnp.int32)
    flags = jnp.concatenate([lit, odd[None], inner[None]])
    side = jnp.stack([odd, inner])
    far_halos, after = [], []
    for part in range(PARTS):
        sent = pack(side, state, wind, True, SCALE, part, 1, after).astype(jnp.float16)
        sent = lax.optimization_barrier(sent)
        after = [sent[0, :8].astype(jnp.float32)]
        far_halos.append(lax.ppermute(sent, "lat", far))
    near_halo = lax.ppermute(pack(side, state, wind, False, 1.0, 0, PARTS, after), "lat", near)
    w1, w2 = w_first.T, w_second.T
    wide_bias = jnp.broadcast_to(bias[:, None], (bias.shape[0], state.shape[3] // PARTS))
    shared = (sunlight, wide_bias, remap, w1, w2)
    fast, unscale = compute(False, 0, flags, state, wind, near_halo, *shared)
    out = None
    for part in range(PARTS):
        halo = far_halos[part].astype(jnp.float32) * unscale[0, 0]
        out = compute(True, part, flags, state, wind, halo, *shared, fast=fast, before=out)
    return out


def solution(mesh):
    placed = (
        P("member", None, "lat", None),
        P("member", "lat", None),
        P(("member", "lat"), None),
        P(("member", "lat"), None),
        P(),
        P(),
        P(),
        P(),
    )
    return jax.shard_map(
        shards,
        mesh=mesh,
        in_specs=placed,
        out_specs=P("member", None, "lat", None),
        check_vma=False,
    )
```

```python
import functools

import jax
import jax.numpy as jnp
from jax import lax
from jax.experimental import pallas as pl
from jax.experimental.pallas import tpu as pltpu
from jax.sharding import PartitionSpec as P

STEPS = 2
REACH = 2 * STEPS
SCALE = 4096.0
FACES = 3
PARTS = 2
CHUNKS = 4
TILES = 4
MIB = 1 << 20


def pack_kernel(flags, state_ref, wind_ref, own_ref, near_ref, *far_refs):
    fields, levels, parts, rows, width = state_ref.shape
    flat = state_ref.reshape(fields * levels * parts * rows, width)
    winds = wind_ref.reshape(levels * parts * rows, width)
    odd = flags[0]
    for part in range(parts):
        for j in range(rows):
            for f in range(fields):
                start = (f * levels * parts + part) * rows + j
                own_ref[part, j * fields + f] = flat[pl.ds(start, levels, stride=parts * rows), :]
            start = part * rows + j
            own_ref[part, rows * fields + j] = winds[pl.ds(start, levels, stride=parts * rows), :]

    def send(upward):
        state_row = rows - REACH if upward else 0
        wind_row = rows - FACES if upward else 0

        def slab(part, n):
            if n < REACH * fields:
                return own_ref[part, state_row * fields + n]
            return own_ref[part, rows * fields + wind_row + n - REACH * fields]

        return slab

    down, up = send(False), send(True)
    for far_slab, near_slab, chosen in ((up, down, odd == 1), (down, up, odd == 0)):

        @pl.when(chosen)
        def _():
            for part in range(PARTS):
                for n in range(REACH * fields + FACES):
                    far_refs[part][n] = far_slab(part, n) * SCALE
                    near_ref[part, n] = near_slab(part, n)


def parted(x):
    *outer, rows, lons = x.shape
    return jnp.swapaxes(x.reshape(*outer, rows, PARTS, lons // PARTS), -3, -2)


def pack(flags, state, wind):
    fields, levels, rows, lons = state.shape
    width = lons // PARTS
    step = levels // CHUNKS
    sent = REACH * fields + FACES
    own = rows * (fields + 1)
    whole = lambda i, s: (0, 0, i, 0)
    return pl.pallas_call(
        pack_kernel,
        grid_spec=pltpu.PrefetchScalarGridSpec(
            num_scalar_prefetch=1,
            grid=(CHUNKS,),
            in_specs=[
                pl.BlockSpec((fields, step, PARTS, rows, width), lambda i, s: (0, i, 0, 0, 0)),
                pl.BlockSpec((step, PARTS, rows, width), lambda i, s: (i, 0, 0, 0)),
            ],
            out_specs=[
                pl.BlockSpec((PARTS, own, step, width), whole),
                pl.BlockSpec((PARTS, sent, step, width), whole),
            ]
            + [pl.BlockSpec((sent, step, width), lambda i, s: (0, i, 0))] * PARTS,
        ),
        out_shape=[
            jax.ShapeDtypeStruct((PARTS, own, levels, width), jnp.float32),
            jax.ShapeDtypeStruct((PARTS, sent, levels, width), jnp.float32),
        ]
        + [jax.ShapeDtypeStruct((sent, levels, width), jnp.float32)] * PARTS,
        name="pack",
        compiler_params=pltpu.CompilerParams(vmem_limit_bytes=24 * MIB),
        cost_estimate=pl.CostEstimate(flops=10**6, bytes_accessed=18 * 10**6, transcendentals=0),
    )(flags, parted(state), parted(wind))


def limited(left, right):
    return jnp.maximum(jnp.minimum(left, right), 0.0) + jnp.minimum(jnp.maximum(left, right), 0.0)


def advance(q, c, ck, positive, first, last):
    diff = {j: q[j + 1] - q[j] for j in range(first - 2, last + 2)}
    slope = {j: limited(diff[j], diff[j - 1]) for j in range(first - 1, last + 2)}
    flux = {}
    for j in range(first, last + 2):
        flux[j] = c[j] * jnp.where(positive[j], q[j - 1], q[j]) + ck[j] * jnp.where(
            positive[j], slope[j - 1], slope[j]
        )
    return {j: q[j] - (flux[j + 1] - flux[j]) for j in range(first, last + 1)}


def gelu(v):
    inner = v * (0.7978845608028654 + (0.7978845608028654 * 0.044715) * (v * v))
    half = 0.5 * v
    return (half + half * jnp.tanh(inner)).astype(jnp.bfloat16)


def advect_rows(north, inner, rows, fields, own_ref, halo, adv, offset):
    chunk = own_ref.shape[2]
    slabs = REACH * fields
    first = 0 if north else rows - REACH
    last = first + REACH - 1

    @pl.loop(0, chunk // 8)
    def _(t):
        here = pl.ds(pl.multiple_of(t * 8, 8), 8)
        there = pl.ds(pl.multiple_of(offset + t * 8, 8), 8)
        c = {}
        for j in range(first - 2, last + 4):
            if j < 0:
                c[j] = halo(slabs + FACES + j, here)
            elif j < rows:
                c[j] = own_ref[0, rows * fields + j, here, :]
            else:
                c[j] = halo(slabs + j - rows, here)
        positive = {j: v > 0.0 for j, v in c.items()}
        ck = {j: 0.5 * (jnp.abs(v) - v * v) for j, v in c.items()}
        for f in range(fields):
            q = {}
            for j in range(first - REACH, last + REACH + 1):
                if j < 0:
                    q[j] = halo((j + REACH) * fields + f, here)
                elif j < rows:
                    q[j] = own_ref[0, j * fields + f, here, :]
                else:
                    q[j] = halo((j - rows) * fields + f, here)
            q = advance(q, c, ck, positive, first - 2, last + 2)
            if north:
                q[-1] = q[-1] * inner
                q[-2] = q[-2] * inner
            q = advance(q, c, ck, positive, first, last)
            for j in range(REACH):
                adv[j, f, there, :] = q[first + j]


def main_kernel(slow, part, rows, flags, own_ref, halo_ref, sun_ref, bias_ref, remap_ref, w1_hbm, w2_hbm, *rest):
    if slow:
        out_hbm, adv, x16, w1, w2, sems, result = rest[-7:]
        fast_ref = rest[0]
    else:
        out_ref, unscale_ref, adv, x16, w1, w2, sems = rest[-7:]
        unscale_ref[0] = 1.0 / SCALE
    half = pl.program_id(0)
    step_id = pl.program_id(1)
    chunk = own_ref.shape[2]
    reach, fields, levels, lons = adv.shape
    load_1 = pltpu.make_async_copy(w1_hbm, w1, sems.at[0])
    load_2 = pltpu.make_async_copy(w2_hbm, w2, sems.at[1])
    odd = flags[flags.shape[0] - 2]
    north = 1 - odd if slow else odd
    inner = jnp.where(flags[flags.shape[0] - 1] > 0, 1.0, 0.0)
    offset = step_id * chunk

    def halo(n, here):
        return halo_ref[n, here, :] if slow else halo_ref[0, n, here, :]

    @pl.when((step_id == 0) & (half == 0))
    def _():
        load_1.start()
        load_2.start()

    @pl.when((step_id < CHUNKS) & (north == 1))
    def _():
        advect_rows(True, inner, rows, fields, own_ref, halo, adv, offset)

    @pl.when((step_id < CHUNKS) & (north == 0))
    def _():
        advect_rows(False, inner, rows, fields, own_ref, halo, adv, offset)

    @pl.when((step_id == CHUNKS) & (half == 0))
    def _():
        load_1.wait()
        load_2.wait()

    @pl.when(step_id == CHUNKS)
    def _():
        base = (1 - north) * (rows - REACH)
        if slow:
            flat_out = result.reshape(fields * levels * rows, lons)
            fast_base = north * (rows - REACH)
            columns = pl.ds(part * lons, lons)
            heated = pl.ds(0, 1)
            others = pl.ds(1, fields - 1)
            store_others = pltpu.make_async_copy(
                result.at[others], out_hbm.at[others, :, :, columns], sems.at[2])
            store_heated = pltpu.make_async_copy(
                result.at[heated], out_hbm.at[heated, :, :, columns], sems.at[3])

        def put(k, f, values):
            if slow:
                flat_out[pl.ds(f * levels * rows + base + k, levels, stride=rows), :] = values
            else:
                out_ref[0, k, f] = values

        remap = remap_ref[...]
        r_high = remap.astype(jnp.bfloat16)
        r_low = (remap - r_high.astype(jnp.float32)).astype(jnp.bfloat16)
        r_all = jnp.concatenate([r_high, r_low, r_high], axis=1)
        hidden_size = w1.shape[0]
        tile = hidden_size // TILES

        for f in range(fields):
            for pair in range(REACH // 2):
                a, b = 2 * pair, 2 * pair + 1
                x = jnp.concatenate([adv[a, f], adv[b, f]], axis=1)
                high = x.astype(jnp.bfloat16)
                low = (x - high.astype(jnp.float32)).astype(jnp.bfloat16)
                stacked = jnp.concatenate([high, high, low], axis=0)
                y = jnp.dot(r_all, stacked, preferred_element_type=jnp.float32)
                x16[pair, pl.ds(f * levels, levels), :] = y.astype(jnp.bfloat16)
                if f == 0:
                    adv[a, 0] = y[:, :lons]
                    adv[b, 0] = y[:, lons:]
                else:
                    put(a, f, y[:, :lons])
                    put(b, f, y[:, lons:])
        if slow:
            for k in range(REACH):
                for f in range(fields):
                    place = pl.ds(f * levels * rows + fast_base + k, levels, stride=rows)
                    flat_out[place, :] = fast_ref[0, k, f]
            store_others.start()

        for pair in range(REACH // 2):
            a, b = 2 * pair, 2 * pair + 1
            lit_a = flags[PARTS * (base + a) + part + half]
            lit_b = flags[PARTS * (base + b) + part + half]

            @pl.when(lit_a + lit_b > 0)
            def _():
                inputs = x16[pair]

                def layer(t):
                    z = jnp.dot(w1[pl.ds(t * tile, tile), :], inputs,
                                preferred_element_type=jnp.float32)
                    wide = bias_ref[pl.ds(t * tile, tile), :]
                    return z + jnp.concatenate([wide, wide], axis=1)

                net = jnp.zeros((levels, 2 * lons), jnp.float32)
                z = layer(0)
                for t in range(TILES):
                    later = layer(t + 1) if t < TILES - 1 else None
                    net = net + jnp.dot(w2[:, pl.ds(t * tile, tile)], gelu(z),
                                        preferred_element_type=jnp.float32)
                    z = later
                for k, lit, values in ((a, lit_a, net[:, :lons]), (b, lit_b, net[:, lons:])):
                    weight = sun_ref[pl.ds(base + k, 1), :] * jnp.where(lit > 0, 1.0, 0.0)
                    adv[k, 0] = adv[k, 0] + weight * values

        for k in range(REACH):
            put(k, 0, adv[k, 0])
        if slow:
            store_heated.start()
            store_others.wait()
            store_heated.wait()


def compute(slow, part, flags, own, halo, sunlight, bias, remap, w1, w2, fast=None, before=None):
    rows, lons = sunlight.shape
    levels, width = own.shape[2:]
    fields = own.shape[1] // rows - 1
    step = levels // CHUNKS
    last = CHUNKS - 1
    hidden_size = w1.shape[0]
    any_spec = pl.BlockSpec(memory_space=pl.ANY)
    halves = 1 if slow else PARTS
    if slow:
        halo_spec = pl.BlockSpec((halo.shape[0], step, width), lambda h, i, s: (0, jnp.minimum(i, last), 0))
    else:
        halo_spec = pl.BlockSpec((1, halo.shape[1], step, width), lambda h, i, s: (h, 0, jnp.minimum(i, last), 0))
    in_specs = [
        pl.BlockSpec((1, own.shape[1], step, width), lambda h, i, s: (part + h, 0, jnp.minimum(i, last), 0)),
        halo_spec,
        pl.BlockSpec((rows, width), lambda h, i, s: (0, part + h)),
        pl.BlockSpec((hidden_size, width), lambda h, i, s: (0, 0)),
        pl.BlockSpec((levels, levels), lambda h, i, s: (0, 0)),
        any_spec,
        any_spec,
    ]
    operands = [flags, own, halo, sunlight, bias, remap, w1, w2]
    scratch = [
        pltpu.VMEM((REACH, fields, levels, width), jnp.float32),
        pltpu.VMEM((REACH // 2, fields * levels, 2 * width), jnp.bfloat16),
        pltpu.VMEM(w1.shape, jnp.bfloat16),
        pltpu.VMEM(w2.shape, jnp.bfloat16),
        pltpu.SemaphoreType.DMA((4,)),
    ]
    aliases = {}
    if slow:
        in_specs.append(pl.BlockSpec((1, REACH, fields, levels, width), lambda h, i, s: (part, 0, 0, 0, 0)))
        operands.append(fast)
        out_spec = any_spec
        out_shape = jax.ShapeDtypeStruct((fields, levels, rows, lons), jnp.float32)
        scratch.append(pltpu.VMEM((fields, levels, rows, width), jnp.float32))
        if before is not None:
            in_specs.append(any_spec)
            operands.append(before)
            aliases = {len(operands) - 1: 0}
    else:
        out_spec = [
            pl.BlockSpec((1, REACH, fields, levels, width), lambda h, i, s: (h, 0, 0, 0, 0)),
            pl.BlockSpec(memory_space=pltpu.SMEM),
        ]
        out_shape = [
            jax.ShapeDtypeStruct((PARTS, REACH, fields, levels, width), jnp.float32),
            jax.ShapeDtypeStruct((1,), jnp.float32),
        ]
    return pl.pallas_call(
        functools.partial(main_kernel, slow, part, rows),
        grid_spec=pltpu.PrefetchScalarGridSpec(
            num_scalar_prefetch=1,
            grid=(halves, CHUNKS + 1),
            in_specs=in_specs,
            out_specs=out_spec,
            scratch_shapes=scratch,
        ),
        out_shape=out_shape,
        input_output_aliases=aliases,
        name="slow_rows" if slow else "fast_rows",
        compiler_params=pltpu.CompilerParams(vmem_limit_bytes=36 * MIB),
        cost_estimate=pl.CostEstimate(
            flops=2 * 10**9 * halves, bytes_accessed=6 * 10**6 * halves, transcendentals=10**6 * halves
        ),
    )(*operands)


def shards(state, wind, sunlight, day_list, w_first, bias, w_second, remap):
    count = lax.axis_size("lat")
    near = [(i, i ^ 1) for i in range(count) if i ^ 1 < count]
    far = [(i, i + 1) for i in range(1, count - 1, 2)]
    far = far + [(j, i) for i, j in far]
    index = lax.axis_index("lat")
    blocks = day_list.shape[1]
    block_ids = jnp.arange(blocks, dtype=jnp.int32)
    lit = jnp.any(day_list[0][None, :] == block_ids[:, None], axis=1).astype(jnp.int32)
    odd = (index % 2).astype(jnp.int32)
    inner = (index > 0).astype(jnp.int32)
    flags = jnp.concatenate([lit, odd[None], inner[None]])
    side = jnp.stack([odd, inner])
    own, near_sent, *far_sent = pack(side, state, wind)
    far_halos = [lax.ppermute(sent.astype(jnp.float16), "lat", far) for sent in far_sent]
    near_halo = lax.ppermute(near_sent, "lat", near)
    w1, w2 = w_first.T, w_second.T
    wide_bias = jnp.broadcast_to(bias[:, None], (bias.shape[0], state.shape[3] // PARTS))
    shared = (sunlight, wide_bias, remap, w1, w2)
    fast, unscale = compute(False, 0, flags, own, near_halo, *shared)
    out = None
    for part in range(PARTS):
        halo = far_halos[part].astype(jnp.float32) * unscale[0]
        out = compute(True, part, flags, own, halo, *shared, fast=fast, before=out)
    return out


def solution(mesh):
    placed = (
        P("member", None, "lat", None),
        P("member", "lat", None),
        P(("member", "lat"), None),
        P(("member", "lat"), None),
        P(),
        P(),
        P(),
        P(),
    )
    return jax.shard_map(
        shards,
        mesh=mesh,
        in_specs=placed,
        out_specs=P("member", None, "lat", None),
        check_vma=False,
    )
```

```python
import functools

import jax
import jax.numpy as jnp
from jax import lax
from jax.experimental import pallas as pl
from jax.experimental.pallas import tpu as pltpu
from jax.sharding import PartitionSpec as P

STEPS = 2
REACH = 2 * STEPS
SCALE = 4096.0
FACES = 3
PARTS = 2
CHUNKS = 4
TILES = 4
MIB = 1 << 20


def pack_kernel(flags, state_ref, wind_ref, near_ref, far_ref):
    fields, levels, parts, rows, width = state_ref.shape
    flat = state_ref.reshape(fields * levels * parts * rows, width)
    winds = wind_ref.reshape(levels * parts * rows, width)
    odd = flags[0]
    stride = parts * rows
    for ref, scale, upward in ((far_ref, SCALE, odd), (near_ref, 1.0, 1 - odd)):
        for part in range(parts):
            for k in range(REACH):
                for f in range(fields):
                    start = (f * levels * parts + part) * rows + upward * (rows - REACH) + k
                    ref[part, k * fields + f] = flat[pl.ds(start, levels, stride=stride), :] * scale
            for k in range(FACES):
                start = part * rows + upward * (rows - FACES) + k
                ref[part, REACH * fields + k] = winds[pl.ds(start, levels, stride=stride), :] * scale


def parted(x):
    *outer, rows, lons = x.shape
    return jnp.swapaxes(x.reshape(*outer, rows, PARTS, lons // PARTS), -3, -2)


def pack(flags, state, wind):
    fields, levels, parts, rows, width = state.shape
    step = levels // CHUNKS
    sent = REACH * fields + FACES
    out = jax.ShapeDtypeStruct((parts, sent, levels, width), jnp.float32)
    out_spec = pl.BlockSpec((parts, sent, step, width), lambda i, s: (0, 0, i, 0))
    return pl.pallas_call(
        pack_kernel,
        grid_spec=pltpu.PrefetchScalarGridSpec(
            num_scalar_prefetch=1,
            grid=(CHUNKS,),
            in_specs=[
                pl.BlockSpec((fields, step, parts, rows, width), lambda i, s: (0, i, 0, 0, 0)),
                pl.BlockSpec((step, parts, rows, width), lambda i, s: (i, 0, 0, 0)),
            ],
            out_specs=[out_spec, out_spec],
        ),
        out_shape=[out, out],
        name="pack",
        compiler_params=pltpu.CompilerParams(vmem_limit_bytes=60 * MIB),
        cost_estimate=pl.CostEstimate(flops=10**6, bytes_accessed=12 * 10**6, transcendentals=0),
    )(flags, state, wind)


def limited(left, right):
    return jnp.maximum(jnp.minimum(left, right), 0.0) + jnp.minimum(jnp.maximum(left, right), 0.0)


def advance(q, c, ck, positive, first, last):
    diff = {j: q[j + 1] - q[j] for j in range(first - 2, last + 2)}
    slope = {j: limited(diff[j], diff[j - 1]) for j in range(first - 1, last + 2)}
    flux = {}
    for j in range(first, last + 2):
        flux[j] = c[j] * jnp.where(positive[j], q[j - 1], q[j]) + ck[j] * jnp.where(
            positive[j], slope[j - 1], slope[j]
        )
    return {j: q[j] - (flux[j + 1] - flux[j]) for j in range(first, last + 1)}


def gelu(v):
    inner = v * (0.7978845608028654 + (0.7978845608028654 * 0.044715) * (v * v))
    half = 0.5 * v
    return (half + half * jnp.tanh(inner)).astype(jnp.bfloat16)


def advect_rows(north, inner, state_ref, wind_ref, halo_ref, adv, offset):
    fields, chunk, parts, rows, lons = state_ref.shape
    slabs = REACH * fields
    stride = parts * rows
    flat = state_ref.reshape(fields * chunk * stride, lons)
    winds = wind_ref.reshape(chunk * stride, lons)
    first = 0 if north else rows - REACH
    last = first + REACH - 1

    @pl.loop(0, parts * chunk // 8)
    def _(n):
        part = n % parts
        t = n // parts
        here = pl.ds(pl.multiple_of(t * 8, 8), 8)
        there = pl.ds(pl.multiple_of(offset + t * 8, 8), 8)
        start = (t * 8 * parts + part) * rows
        c = {}
        for j in range(first - 2, last + 4):
            if j < 0:
                c[j] = halo_ref[part, slabs + FACES + j, here, :]
            elif j < rows:
                c[j] = winds[pl.ds(start + j, 8, stride=stride), :]
            else:
                c[j] = halo_ref[part, slabs + j - rows, here, :]
        positive = {j: v > 0.0 for j, v in c.items()}
        ck = {j: 0.5 * (jnp.abs(v) - v * v) for j, v in c.items()}
        for f in range(fields):
            q = {}
            for j in range(first - REACH, last + REACH + 1):
                if j < 0:
                    q[j] = halo_ref[part, (j + REACH) * fields + f, here, :]
                elif j < rows:
                    q[j] = flat[pl.ds(f * chunk * stride + start + j, 8, stride=stride), :]
                else:
                    q[j] = halo_ref[part, (j - rows) * fields + f, here, :]
            q = advance(q, c, ck, positive, first - 2, last + 2)
            if north:
                q[-1] = q[-1] * inner
                q[-2] = q[-2] * inner
            q = advance(q, c, ck, positive, first, last)
            for j in range(REACH):
                adv[part, j, f, there, :] = q[first + j]


def main_kernel(slow, flags, state_ref, wind_ref, halo_ref, sun_ref, bias_ref, remap_ref, w1_hbm, w2_hbm, *rest):
    if slow:
        fast_ref, out_hbm, adv, x16, w1, w2, sems, result = rest
    else:
        out_ref, unscale_ref, adv, x16, w1, w2, sems = rest
        unscale_ref[0] = 1.0 / SCALE
    step_id = pl.program_id(0)
    rows = state_ref.shape[3]
    parts, reach, fields, levels, lons = adv.shape
    chunk = state_ref.shape[1]
    load_1 = pltpu.make_async_copy(w1_hbm, w1, sems.at[0])
    load_2 = pltpu.make_async_copy(w2_hbm, w2, sems.at[1])
    odd = flags[flags.shape[0] - 2]
    north = 1 - odd if slow else odd
    inner = jnp.where(flags[flags.shape[0] - 1] > 0, 1.0, 0.0)
    offset = step_id * chunk

    @pl.when(step_id == 0)
    def _():
        load_1.start()
        load_2.start()

    @pl.when((step_id < CHUNKS) & (north == 1))
    def _():
        advect_rows(True, inner, state_ref, wind_ref, halo_ref, adv, offset)

    @pl.when((step_id < CHUNKS) & (north == 0))
    def _():
        advect_rows(False, inner, state_ref, wind_ref, halo_ref, adv, offset)

    @pl.when(step_id == CHUNKS)
    def _():
        load_1.wait()
        load_2.wait()
        base = (1 - north) * (rows - reach)
        stride = parts * rows
        if slow:
            flat_out = result.reshape(fields * levels * stride, lons)
            fast_base = north * (rows - reach)
            heated = pl.ds(0, 1)
            others = pl.ds(1, fields - 1)
            store_others = pltpu.make_async_copy(result.at[others], out_hbm.at[others], sems.at[2])
            store_heated = pltpu.make_async_copy(result.at[heated], out_hbm.at[heated], sems.at[3])

        def put(part, k, f, values):
            if slow:
                start = (f * levels * parts + part) * rows + base + k
                flat_out[pl.ds(start, levels, stride=stride), :] = values
            else:
                out_ref[part, k, f] = values

        remap = remap_ref[...]
        r_high = remap.astype(jnp.bfloat16)
        r_low = (remap - r_high.astype(jnp.float32)).astype(jnp.bfloat16)
        r_all = jnp.concatenate([r_high, r_low, r_high], axis=1)
        hidden_size = w1.shape[0]
        tile = hidden_size // TILES
        pairs = [(part, pair) for part in range(parts) for pair in range(reach // 2)]

        for f in range(fields):
            for n, (part, pair) in enumerate(pairs):
                a, b = 2 * pair, 2 * pair + 1
                x = jnp.concatenate([adv[part, a, f], adv[part, b, f]], axis=1)
                high = x.astype(jnp.bfloat16)
                low = (x - high.astype(jnp.float32)).astype(jnp.bfloat16)
                stacked = jnp.concatenate([high, high, low], axis=0)
                y = jnp.dot(r_all, stacked, preferred_element_type=jnp.float32)
                x16[n, pl.ds(f * levels, levels), :] = y.astype(jnp.bfloat16)
                for k, values in ((a, y[:, :lons]), (b, y[:, lons:])):
                    if f == 0:
                        adv[part, k, 0] = values
                    else:
                        put(part, k, f, values)
        if slow:
            for part in range(parts):
                for k in range(reach):
                    for f in range(fields):
                        start = (f * levels * parts + part) * rows + fast_base + k
                        flat_out[pl.ds(start, levels, stride=stride), :] = fast_ref[part, k, f]
            store_others.start()

        for n, (part, pair) in enumerate(pairs):
            a, b = 2 * pair, 2 * pair + 1
            lit_a = flags[parts * (base + a) + part]
            lit_b = flags[parts * (base + b) + part]

            @pl.when(lit_a + lit_b > 0)
            def _():
                inputs = x16[n]

                def layer(t):
                    z = jnp.dot(w1[pl.ds(t * tile, tile), :], inputs,
                                preferred_element_type=jnp.float32)
                    wide = bias_ref[pl.ds(t * tile, tile), :]
                    return z + jnp.concatenate([wide, wide], axis=1)

                net = jnp.zeros((levels, 2 * lons), jnp.float32)
                z = layer(0)
                for t in range(TILES):
                    later = layer(t + 1) if t < TILES - 1 else None
                    net = net + jnp.dot(w2[:, pl.ds(t * tile, tile)], gelu(z),
                                        preferred_element_type=jnp.float32)
                    z = later
                for k, lit, values in ((a, lit_a, net[:, :lons]), (b, lit_b, net[:, lons:])):
                    sun = sun_ref[part, pl.ds(base + k, 1), :]
                    weight = sun * jnp.where(lit > 0, 1.0, 0.0)
                    adv[part, k, 0] = adv[part, k, 0] + weight * values

        for part in range(parts):
            for k in range(reach):
                put(part, k, 0, adv[part, k, 0])
        if slow:
            store_heated.start()
            store_others.wait()
            store_heated.wait()


def compute(slow, flags, state, wind, halo, sunlight, bias, remap, w1, w2, fast=None):
    fields, levels, parts, rows, width = state.shape
    step = levels // CHUNKS
    last = CHUNKS - 1
    any_spec = pl.BlockSpec(memory_space=pl.ANY)
    in_specs = [
        pl.BlockSpec((fields, step, parts, rows, width), lambda i, s: (0, jnp.minimum(i, last), 0, 0, 0)),
        pl.BlockSpec((step, parts, rows, width), lambda i, s: (jnp.minimum(i, last), 0, 0, 0)),
        pl.BlockSpec((parts, halo.shape[1], step, width), lambda i, s: (0, 0, jnp.minimum(i, last), 0)),
        pl.BlockSpec(sunlight.shape, lambda i, s: (0, 0, 0)),
        pl.BlockSpec(bias.shape, lambda i, s: (0, 0)),
        pl.BlockSpec(remap.shape, lambda i, s: (0, 0)),
        any_spec,
        any_spec,
    ]
    operands = [flags, state, wind, halo, sunlight, bias, remap, w1, w2]
    kept = (parts, REACH, fields, levels, width)
    scratch = [
        pltpu.VMEM(kept, jnp.float32),
        pltpu.VMEM((parts * REACH // 2, fields * levels, 2 * width), jnp.bfloat16),
        pltpu.VMEM(w1.shape, jnp.bfloat16),
        pltpu.VMEM(w2.shape, jnp.bfloat16),
        pltpu.SemaphoreType.DMA((4,)),
    ]
    if slow:
        in_specs.append(pl.BlockSpec(kept, lambda i, s: (0, 0, 0, 0, 0)))
        operands.append(fast)
        out_spec = any_spec
        out_shape = jax.ShapeDtypeStruct(state.shape, jnp.float32)
        scratch.append(pltpu.VMEM(state.shape, jnp.float32))
    else:
        out_spec = [
            pl.BlockSpec(kept, lambda i, s: (0, 0, 0, 0, 0)),
            pl.BlockSpec(memory_space=pltpu.SMEM),
        ]
        out_shape = [
            jax.ShapeDtypeStruct(kept, jnp.float32),
            jax.ShapeDtypeStruct((1,), jnp.float32),
        ]
    return pl.pallas_call(
        functools.partial(main_kernel, slow),
        grid_spec=pltpu.PrefetchScalarGridSpec(
            num_scalar_prefetch=1,
            grid=(CHUNKS + 1,),
            in_specs=in_specs,
            out_specs=out_spec,
            scratch_shapes=scratch,
        ),
        out_shape=out_shape,
        name="slow_rows" if slow else "fast_rows",
        compiler_params=pltpu.CompilerParams(vmem_limit_bytes=56 * MIB),
        cost_estimate=pl.CostEstimate(flops=4 * 10**9, bytes_accessed=12 * 10**6, transcendentals=2 * 10**6),
    )(*operands)


def shards(state, wind, sunlight, day_list, w_first, bias, w_second, remap):
    count = lax.axis_size("lat")
    near = [(i, i ^ 1) for i in range(count) if i ^ 1 < count]
    far = [(i, i + 1) for i in range(1, count - 1, 2)]
    far = far + [(j, i) for i, j in far]
    index = lax.axis_index("lat")
    blocks = day_list.shape[1]
    block_ids = jnp.arange(blocks, dtype=jnp.int32)
    lit = jnp.any(day_list[0][None, :] == block_ids[:, None], axis=1).astype(jnp.int32)
    odd = (index % 2).astype(jnp.int32)
    inner = (index > 0).astype(jnp.int32)
    flags = jnp.concatenate([lit, odd[None], inner[None]])
    side = jnp.stack([odd, inner])
    parts_state, parts_wind = parted(state), parted(wind)
    near_sent, far_sent = pack(side, parts_state, parts_wind)
    far_halo = lax.ppermute(far_sent.astype(jnp.float16), "lat", far)
    near_halo = lax.ppermute(near_sent, "lat", near)
    w1, w2 = w_first.T, w_second.T
    wide_bias = jnp.broadcast_to(bias[:, None], (bias.shape[0], state.shape[3] // PARTS))
    shared = (parted(sunlight), wide_bias, remap, w1, w2)
    fast, unscale = compute(False, flags, parts_state, parts_wind, near_halo, *shared)
    far_halo = far_halo.astype(jnp.float32) * unscale[0]
    out = compute(True, flags, parts_state, parts_wind, far_halo, *shared, fast=fast)
    return jnp.swapaxes(out, 2, 3).reshape(state.shape)


def solution(mesh):
    placed = (
        P("member", None, "lat", None),
        P("member", "lat", None),
        P(("member", "lat"), None),
        P(("member", "lat"), None),
        P(),
        P(),
        P(),
        P(),
    )
    return jax.shard_map(
        shards,
        mesh=mesh,
        in_specs=placed,
        out_specs=P("member", None, "lat", None),
        check_vma=False,
    )
```

```python
import functools

import jax
import jax.numpy as jnp
from jax import lax
from jax.experimental import pallas as pl
from jax.experimental.pallas import tpu as pltpu
from jax.sharding import PartitionSpec as P

STEPS = 2
REACH = 2 * STEPS
SCALE = 4096.0
FACES = 3
PARTS = 2
CHUNKS = 4
TILES = 4
MIB = 1 << 20


def pack_kernel(flags, state_ref, wind_ref, own_ref, near_ref, *far_refs):
    fields, levels, parts, rows, width = state_ref.shape
    flat = state_ref.reshape(fields * levels * parts * rows, width)
    winds = wind_ref.reshape(levels * parts * rows, width)
    odd = flags[0]
    for part in range(parts):
        for j in range(rows):
            for f in range(fields):
                start = (f * levels * parts + part) * rows + j
                own_ref[part, j * fields + f] = flat[pl.ds(start, levels, stride=parts * rows), :]
            start = part * rows + j
            own_ref[part, rows * fields + j] = winds[pl.ds(start, levels, stride=parts * rows), :]

    def send(upward):
        state_row = rows - REACH if upward else 0
        wind_row = rows - FACES if upward else 0

        def slab(part, n):
            if n < REACH * fields:
                return own_ref[part, state_row * fields + n]
            return own_ref[part, rows * fields + wind_row + n - REACH * fields]

        return slab

    down, up = send(False), send(True)
    for far_slab, near_slab, chosen in ((up, down, odd == 1), (down, up, odd == 0)):

        @pl.when(chosen)
        def _():
            for part in range(PARTS):
                for n in range(REACH * fields + FACES):
                    far_refs[part][n] = far_slab(part, n) * SCALE
                    near_ref[part, n] = near_slab(part, n)


def parted(x):
    *outer, rows, lons = x.shape
    return jnp.swapaxes(x.reshape(*outer, rows, PARTS, lons // PARTS), -3, -2)


def pack(flags, state, wind):
    fields, levels, rows, lons = state.shape
    width = lons // PARTS
    step = levels // CHUNKS
    sent = REACH * fields + FACES
    own = rows * (fields + 1)
    whole = lambda i, s: (0, 0, i, 0)
    return pl.pallas_call(
        pack_kernel,
        grid_spec=pltpu.PrefetchScalarGridSpec(
            num_scalar_prefetch=1,
            grid=(CHUNKS,),
            in_specs=[
                pl.BlockSpec((fields, step, PARTS, rows, width), lambda i, s: (0, i, 0, 0, 0)),
                pl.BlockSpec((step, PARTS, rows, width), lambda i, s: (i, 0, 0, 0)),
            ],
            out_specs=[
                pl.BlockSpec((PARTS, own, step, width), whole),
                pl.BlockSpec((PARTS, sent, step, width), whole),
            ]
            + [pl.BlockSpec((sent, step, width), lambda i, s: (0, i, 0))] * PARTS,
        ),
        out_shape=[
            jax.ShapeDtypeStruct((PARTS, own, levels, width), jnp.float32),
            jax.ShapeDtypeStruct((PARTS, sent, levels, width), jnp.float32),
        ]
        + [jax.ShapeDtypeStruct((sent, levels, width), jnp.float32)] * PARTS,
        name="pack",
        compiler_params=pltpu.CompilerParams(vmem_limit_bytes=14 * MIB),
        cost_estimate=pl.CostEstimate(flops=10**6, bytes_accessed=18 * 10**6, transcendentals=0),
    )(flags, parted(state), parted(wind))


def limited(left, right):
    return jnp.maximum(jnp.minimum(left, right), 0.0) + jnp.minimum(jnp.maximum(left, right), 0.0)


def advance(q, c, ck, positive, first, last):
    diff = {j: q[j + 1] - q[j] for j in range(first - 2, last + 2)}
    slope = {j: limited(diff[j], diff[j - 1]) for j in range(first - 1, last + 2)}
    flux = {}
    for j in range(first, last + 2):
        flux[j] = c[j] * jnp.where(positive[j], q[j - 1], q[j]) + ck[j] * jnp.where(
            positive[j], slope[j - 1], slope[j]
        )
    return {j: q[j] - (flux[j + 1] - flux[j]) for j in range(first, last + 1)}


def gelu(v):
    inner = v * (0.7978845608028654 + (0.7978845608028654 * 0.044715) * (v * v))
    half = 0.5 * v
    return (half + half * jnp.tanh(inner)).astype(jnp.bfloat16)


def advect_rows(north, inner, rows, fields, own_ref, halo, adv, offset):
    chunk = own_ref.shape[2]
    slabs = REACH * fields
    first = 0 if north else rows - REACH
    last = first + REACH - 1

    @pl.loop(0, chunk // 8)
    def _(t):
        here = pl.ds(pl.multiple_of(t * 8, 8), 8)
        there = pl.ds(pl.multiple_of(offset + t * 8, 8), 8)
        c = {}
        for j in range(first - 2, last + 4):
            if j < 0:
                c[j] = halo(slabs + FACES + j, here)
            elif j < rows:
                c[j] = own_ref[0, rows * fields + j, here, :]
            else:
                c[j] = halo(slabs + j - rows, here)
        positive = {j: v > 0.0 for j, v in c.items()}
        ck = {j: 0.5 * (jnp.abs(v) - v * v) for j, v in c.items()}
        for f in range(fields):
            q = {}
            for j in range(first - REACH, last + REACH + 1):
                if j < 0:
                    q[j] = halo((j + REACH) * fields + f, here)
                elif j < rows:
                    q[j] = own_ref[0, j * fields + f, here, :]
                else:
                    q[j] = halo((j - rows) * fields + f, here)
            q = advance(q, c, ck, positive, first - 2, last + 2)
            if north:
                q[-1] = q[-1] * inner
                q[-2] = q[-2] * inner
            q = advance(q, c, ck, positive, first, last)
            for j in range(REACH):
                adv[j, f, there, :] = q[first + j]


def main_kernel(slow, part, rows, flags, own_ref, halo_ref, sun_ref, bias_ref, remap_ref, w1_hbm, w2_hbm, *rest):
    if slow:
        out_hbm, adv, x16, w1, w2, sems, result = rest[-7:]
        fast_ref = rest[0]
    else:
        out_ref, unscale_ref, adv, x16, w1, w2, sems = rest[-7:]
        unscale_ref[0] = 1.0 / SCALE
    half = pl.program_id(0)
    step_id = pl.program_id(1)
    chunk = own_ref.shape[2]
    reach, fields, levels, lons = adv.shape
    load_1 = pltpu.make_async_copy(w1_hbm, w1, sems.at[0])
    load_2 = pltpu.make_async_copy(w2_hbm, w2, sems.at[1])
    odd = flags[flags.shape[0] - 2]
    north = 1 - odd if slow else odd
    inner = jnp.where(flags[flags.shape[0] - 1] > 0, 1.0, 0.0)
    offset = step_id * chunk

    def halo(n, here):
        return halo_ref[n, here, :] if slow else halo_ref[0, n, here, :]

    @pl.when((step_id == 0) & (half == 0))
    def _():
        load_1.start()
        load_2.start()

    @pl.when((step_id < CHUNKS) & (north == 1))
    def _():
        advect_rows(True, inner, rows, fields, own_ref, halo, adv, offset)

    @pl.when((step_id < CHUNKS) & (north == 0))
    def _():
        advect_rows(False, inner, rows, fields, own_ref, halo, adv, offset)

    @pl.when((step_id == CHUNKS) & (half == 0))
    def _():
        load_1.wait()
        load_2.wait()

    @pl.when(step_id == CHUNKS)
    def _():
        base = (1 - north) * (rows - REACH)
        if slow:
            flat_out = result.reshape(fields * levels * rows, lons)
            fast_base = north * (rows - REACH)
            columns = pl.ds(part * lons, lons)
            heated = pl.ds(0, 1)
            others = pl.ds(1, fields - 1)
            store_others = pltpu.make_async_copy(
                result.at[others], out_hbm.at[others, :, :, columns], sems.at[2])
            store_heated = pltpu.make_async_copy(
                result.at[heated], out_hbm.at[heated, :, :, columns], sems.at[3])

        def put(k, f, values):
            if slow:
                flat_out[pl.ds(f * levels * rows + base + k, levels, stride=rows), :] = values
            else:
                out_ref[0, k, f] = values

        remap = remap_ref[...]
        r_high = remap.astype(jnp.bfloat16)
        r_low = (remap - r_high.astype(jnp.float32)).astype(jnp.bfloat16)
        r_all = jnp.concatenate([r_high, r_low, r_high], axis=1)
        hidden_size = w1.shape[0]
        tile = hidden_size // TILES

        for f in range(fields):
            for pair in range(REACH // 2):
                a, b = 2 * pair, 2 * pair + 1
                x = jnp.concatenate([adv[a, f], adv[b, f]], axis=1)
                high = x.astype(jnp.bfloat16)
                low = (x - high.astype(jnp.float32)).astype(jnp.bfloat16)
                stacked = jnp.concatenate([high, high, low], axis=0)
                y = jnp.dot(r_all, stacked, preferred_element_type=jnp.float32)
                x16[pair, pl.ds(f * levels, levels), :] = y.astype(jnp.bfloat16)
                if f == 0:
                    adv[a, 0] = y[:, :lons]
                    adv[b, 0] = y[:, lons:]
                else:
                    put(a, f, y[:, :lons])
                    put(b, f, y[:, lons:])
        if slow:
            for k in range(REACH):
                for f in range(fields):
                    place = pl.ds(f * levels * rows + fast_base + k, levels, stride=rows)
                    flat_out[place, :] = fast_ref[0, k, f]
            store_others.start()

        for pair in range(REACH // 2):
            a, b = 2 * pair, 2 * pair + 1
            lit_a = flags[PARTS * (base + a) + part + half]
            lit_b = flags[PARTS * (base + b) + part + half]

            @pl.when(lit_a + lit_b > 0)
            def _():
                inputs = x16[pair]

                def layer(t):
                    z = jnp.dot(w1[pl.ds(t * tile, tile), :], inputs,
                                preferred_element_type=jnp.float32)
                    wide = bias_ref[pl.ds(t * tile, tile), :]
                    return z + jnp.concatenate([wide, wide], axis=1)

                net = jnp.zeros((levels, 2 * lons), jnp.float32)
                z = layer(0)
                for t in range(TILES):
                    later = layer(t + 1) if t < TILES - 1 else None
                    net = net + jnp.dot(w2[:, pl.ds(t * tile, tile)], gelu(z),
                                        preferred_element_type=jnp.float32)
                    z = later
                for k, lit, values in ((a, lit_a, net[:, :lons]), (b, lit_b, net[:, lons:])):
                    weight = sun_ref[pl.ds(base + k, 1), :] * jnp.where(lit > 0, 1.0, 0.0)
                    adv[k, 0] = adv[k, 0] + weight * values

        for k in range(REACH):
            put(k, 0, adv[k, 0])
        if slow:
            store_heated.start()
            store_others.wait()
            store_heated.wait()


def compute(slow, part, flags, own, halo, sunlight, bias, remap, w1, w2, fast=None, before=None):
    rows, lons = sunlight.shape
    levels, width = own.shape[2:]
    fields = own.shape[1] // rows - 1
    step = levels // CHUNKS
    last = CHUNKS - 1
    hidden_size = w1.shape[0]
    any_spec = pl.BlockSpec(memory_space=pl.ANY)
    halves = 1 if slow else PARTS
    if slow:
        halo_spec = pl.BlockSpec((halo.shape[0], step, width), lambda h, i, s: (0, jnp.minimum(i, last), 0))
    else:
        halo_spec = pl.BlockSpec((1, halo.shape[1], step, width), lambda h, i, s: (h, 0, jnp.minimum(i, last), 0))
    in_specs = [
        pl.BlockSpec((1, own.shape[1], step, width), lambda h, i, s: (part + h, 0, jnp.minimum(i, last), 0)),
        halo_spec,
        pl.BlockSpec((rows, width), lambda h, i, s: (0, part + h)),
        pl.BlockSpec((hidden_size, width), lambda h, i, s: (0, 0)),
        pl.BlockSpec((levels, levels), lambda h, i, s: (0, 0)),
        any_spec,
        any_spec,
    ]
    operands = [flags, own, halo, sunlight, bias, remap, w1, w2]
    scratch = [
        pltpu.VMEM((REACH, fields, levels, width), jnp.float32),
        pltpu.VMEM((REACH // 2, fields * levels, 2 * width), jnp.bfloat16),
        pltpu.VMEM(w1.shape, jnp.bfloat16),
        pltpu.VMEM(w2.shape, jnp.bfloat16),
        pltpu.SemaphoreType.DMA((4,)),
    ]
    aliases = {}
    if slow:
        in_specs.append(pl.BlockSpec((1, REACH, fields, levels, width), lambda h, i, s: (part, 0, 0, 0, 0)))
        operands.append(fast)
        out_spec = any_spec
        out_shape = jax.ShapeDtypeStruct((fields, levels, rows, lons), jnp.float32)
        scratch.append(pltpu.VMEM((fields, levels, rows, width), jnp.float32))
        if before is not None:
            in_specs.append(any_spec)
            operands.append(before)
            aliases = {len(operands) - 1: 0}
    else:
        out_spec = [
            pl.BlockSpec((1, REACH, fields, levels, width), lambda h, i, s: (h, 0, 0, 0, 0)),
            pl.BlockSpec(memory_space=pltpu.SMEM),
        ]
        out_shape = [
            jax.ShapeDtypeStruct((PARTS, REACH, fields, levels, width), jnp.float32),
            jax.ShapeDtypeStruct((1,), jnp.float32),
        ]
    return pl.pallas_call(
        functools.partial(main_kernel, slow, part, rows),
        grid_spec=pltpu.PrefetchScalarGridSpec(
            num_scalar_prefetch=1,
            grid=(halves, CHUNKS + 1),
            in_specs=in_specs,
            out_specs=out_spec,
            scratch_shapes=scratch,
        ),
        out_shape=out_shape,
        input_output_aliases=aliases,
        name="slow_rows" if slow else "fast_rows",
        compiler_params=pltpu.CompilerParams(vmem_limit_bytes=22 * MIB),
        cost_estimate=pl.CostEstimate(
            flops=2 * 10**9 * halves, bytes_accessed=6 * 10**6 * halves, transcendentals=10**6 * halves
        ),
    )(*operands)


def shards(state, wind, sunlight, day_list, w_first, bias, w_second, remap):
    count = lax.axis_size("lat")
    near = [(i, i ^ 1) for i in range(count) if i ^ 1 < count]
    far = [(i, i + 1) for i in range(1, count - 1, 2)]
    far = far + [(j, i) for i, j in far]
    index = lax.axis_index("lat")
    blocks = day_list.shape[1]
    block_ids = jnp.arange(blocks, dtype=jnp.int32)
    lit = jnp.any(day_list[0][None, :] == block_ids[:, None], axis=1).astype(jnp.int32)
    odd = (index % 2).astype(jnp.int32)
    inner = (index > 0).astype(jnp.int32)
    flags = jnp.concatenate([lit, odd[None], inner[None]])
    side = jnp.stack([odd, inner])
    own, near_sent, *far_sent = pack(side, state, wind)
    far_halos = [lax.ppermute(sent.astype(jnp.float16), "lat", far) for sent in far_sent]
    near_halo = lax.ppermute(near_sent, "lat", near)
    w1, w2 = w_first.T, w_second.T
    wide_bias = jnp.broadcast_to(bias[:, None], (bias.shape[0], state.shape[3] // PARTS))
    shared = (sunlight, wide_bias, remap, w1, w2)
    fast, unscale = compute(False, 0, flags, own, near_halo, *shared)
    out = None
    for part in range(PARTS):
        halo = far_halos[part].astype(jnp.float32) * unscale[0]
        out = compute(True, part, flags, own, halo, *shared, fast=fast, before=out)
    return out


def solution(mesh):
    placed = (
        P("member", None, "lat", None),
        P("member", "lat", None),
        P(("member", "lat"), None),
        P(("member", "lat"), None),
        P(),
        P(),
        P(),
        P(),
    )
    return jax.shard_map(
        shards,
        mesh=mesh,
        in_specs=placed,
        out_specs=P("member", None, "lat", None),
        check_vma=False,
    )
```
